32 devices in a mesh: row: 8 (over y, x, core), col: 4 (over z).
Axes of the slice: x: 2, y: 2, z: 4, core: 2. Of those that a mesh axis runs over, the one named last changes fastest.
Arguments:
- stem: bfloat16 [8, 4, 1, 512, 2, 512], P('row', 'col'), may hold values from -6 to 6
- branch: bfloat16 [8, 4, 2, 512, 512], P('row', None, None, None, 'col'), may hold values from -0.1875 to 0.1875
Outputs:
- amplitudes: bfloat16 [8, 4, 1, 512, 2, 512], P('row', 'col')
The draws below stay inside these ranges and needn't reach their ends.
All inputs are finite; a program needn't handle non-finite values.
Results may differ from the reference program's by a relative error of at most 0.0075.
Values may be sent and summed in bfloat16 or wider, within the bound.
A program may use at most 64 MiB of HBM per device.

```python
import jax
import jax.numpy as jnp
from jax import lax

ORDER = 512
STEM_ROWS = 1
BUILDS = 4
N_ROW = 8
N_COL = 4


def levels(key, dims, split, least, largest):
    def one(axis_at, parts):
        steps = jax.random.uniform(jax.random.fold_in(jax.random.fold_in(key, 6), axis_at), (parts,), jnp.float32, least / len(split), largest / len(split))
        return jnp.repeat(jnp.exp(steps), dims[axis_at] // parts).reshape((-1,) + (1,) * (len(dims) - axis_at - 1))

    level = one(*split[0])
    for cut in split[1:]:
        level = level * one(*cut)
    return level


def gaussian(own_key, shape, width, limit, cuts=(), held_as=jnp.bfloat16):
    values = jax.random.normal(own_key, shape, jnp.float32) * width
    if len(cuts) > 0:
        values = levels(own_key, shape, cuts, -0.22, 0.18) * values
    return jnp.clip(values, min=-limit, max=limit).astype(held_as)


def setup_inputs(seed: int = 0) -> dict:
    streams_of = jax.random.split(jax.random.key(seed), 3)
    return {
        "stem": gaussian(streams_of[0], (N_ROW, N_COL, STEM_ROWS, ORDER, 2, ORDER), 1.0, 6.0, ((0, 8), (1, 4))),
        "branch": gaussian(streams_of[1], (N_ROW, BUILDS, 2, ORDER, ORDER), (2 * ORDER) ** -0.5, 0.1875, ((0, 8), (4, 4))),
    }


def product_right(left, right):
    return jnp.einsum("...j,kj->...k", left, right, precision=lax.Precision.HIGHEST)


def product_left(left, right):
    return jnp.einsum("ki,...ij->...kj", left, right, precision=lax.Precision.HIGHEST)


def right_apply(block, branch_one):
    real_in = block[..., 0, :].astype(jnp.float32)
    imag_in = block[..., 1, :].astype(jnp.float32)
    real_w = branch_one[0].astype(jnp.float32)
    imag_w = branch_one[1].astype(jnp.float32)
    real_out = product_right(real_in, real_w) - product_right(imag_in, imag_w)
    imag_out = product_right(real_in, imag_w) + product_right(imag_in, real_w)
    return jnp.stack([real_out, imag_out], axis=-2).astype(jnp.bfloat16)


def left_apply(block, branch_one):
    real_in = block[..., :, 0, :].astype(jnp.float32)
    imag_in = block[..., :, 1, :].astype(jnp.float32)
    real_w = branch_one[0].astype(jnp.float32)
    imag_w = branch_one[1].astype(jnp.float32)
    real_out = product_left(real_w, real_in) - product_left(imag_w, imag_in)
    imag_out = product_left(imag_w, real_in) + product_left(real_w, imag_in)
    return jnp.stack([real_out, imag_out], axis=-2).astype(jnp.bfloat16)


def reference(stem, branch):
    row_count = stem.shape[0]
    col_count = stem.shape[1]
    slab_count = stem.shape[2]
    order_size = stem.shape[3]

    def first_step(packed):
        block, branch_row = packed
        return left_apply(right_apply(block, branch_row[1]), branch_row[0])

    step_first = lax.map(first_step, (stem, branch))
    share = order_size // row_count
    moved = step_first.reshape(row_count, col_count, slab_count, row_count, share, 2, order_size)
    moved = jnp.transpose(moved, (3, 1, 2, 0, 4, 5, 6)).reshape(stem.shape)

    def second_step(packed):
        block, branch_row = packed
        return left_apply(right_apply(block, branch_row[3]), branch_row[2])

    step_second = lax.map(second_step, (moved, branch))
    final = step_second.reshape(row_count, col_count, slab_count, order_size, 2, row_count, share)
    final = jnp.transpose(final, (5, 1, 2, 3, 4, 0, 6)).reshape(stem.shape)
    return final
```

```python
import functools

import jax
import jax.numpy as jnp
from jax import lax
from jax.experimental import pallas as pl
from jax.experimental.pallas import tpu as pltpu
from jax.sharding import PartitionSpec as P

MESH = pl.DeviceIdType.MESH
BRANCH_ORDER = (1, 0, 3, 2)
CHUNKS = {1: 1, 0: 1, 3: 1, 2: 2}
MAX_CHUNKS = 2
TAIL_CHUNKS = 2
LANES = 128


def kernel(rows, cols, stem_ref, branch_ref, out_ref,
           stem_v, whole, hcat, hneg, step_v, moved, leave, fin,
           up_send, up_recv, dn_send, dn_recv, own_sem, stem_sem,
           mid_send, mid_recv, mid_own, fin_send, fin_recv, fin_own):
    order = stem_ref.shape[1]
    width = branch_ref.shape[3]
    share = order // rows
    me = lax.axis_index("row")
    z = lax.axis_index("col")
    has_up = z < cols - 1
    has_dn = z > 0

    stem_copy = pltpu.make_async_copy(stem_ref, stem_v, stem_sem)
    stem_copy.start()
    own_copies = {}
    own_lanes = pl.ds(pl.multiple_of(z * width, width), width)
    for b in BRANCH_ORDER:
        own_copies[b] = pltpu.make_async_copy(branch_ref.at[b], whole.at[b, :, :, own_lanes], own_sem.at[b])
        own_copies[b].start()

    barrier = pltpu.get_barrier_semaphore()
    for d in range(1, rows):
        pl.semaphore_signal(barrier, inc=1, device_id={"row": lax.rem(me + d, rows)}, device_id_type=MESH)

    @pl.when(has_up)
    def _():
        pl.semaphore_signal(barrier, inc=1, device_id={"col": z + 1}, device_id_type=MESH)

    @pl.when(has_dn)
    def _():
        pl.semaphore_signal(barrier, inc=1, device_id={"col": z - 1}, device_id_type=MESH)

    pl.semaphore_wait(barrier, rows - 1 + has_up.astype(jnp.int32) + has_dn.astype(jnp.int32))

    def block_at(b, ch, origin):
        step = order // CHUNKS[b]
        lanes = pl.ds(pl.multiple_of(origin * width, width), width)
        return whole.at[b, :, ch * step:(ch + 1) * step, lanes]

    def own_at(b, ch):
        step = order // CHUNKS[b]
        return branch_ref.at[b, :, ch * step:(ch + 1) * step, :]

    def up_copy(b, ch, k, origin, own=False):
        return pltpu.make_async_remote_copy(
            src_ref=own_at(b, ch) if own else block_at(b, ch, origin), dst_ref=block_at(b, ch, origin),
            send_sem=up_send.at[b, ch, k], recv_sem=up_recv.at[b, ch, k],
            device_id={"col": z + 1}, device_id_type=MESH)

    def dn_copy(b, ch, k, origin, own=False):
        return pltpu.make_async_remote_copy(
            src_ref=own_at(b, ch) if own else block_at(b, ch, origin), dst_ref=block_at(b, ch, origin),
            send_sem=dn_send.at[b, ch, k], recv_sem=dn_recv.at[b, ch, k],
            device_id={"col": z - 1}, device_id_type=MESH)

    def send_own(b):
        for ch in range(CHUNKS[b]):
            @pl.when(has_up)
            def _():
                up_copy(b, ch, 0, z, own=True).start()

            @pl.when(has_dn)
            def _():
                dn_copy(b, ch, 0, z, own=True).start()

    def collect(b, ch):
        for k in range(cols - 1):
            @pl.when(z - 1 - k >= 0)
            def _():
                up_copy(b, ch, k, z - 1 - k).wait_recv()

                @pl.when(has_up)
                def _():
                    up_copy(b, ch, k + 1, z - 1 - k).start()

            @pl.when(z + 1 + k <= cols - 1)
            def _():
                dn_copy(b, ch, k, z + 1 + k).wait_recv()

                @pl.when(has_dn)
                def _():
                    dn_copy(b, ch, k + 1, z + 1 + k).start()

    def nt(a, w):
        return lax.dot_general(a, w, (((1,), (1,)), ((), ())), preferred_element_type=jnp.float32)

    def nn(w, a):
        return lax.dot_general(w, a, (((1,), (0,)), ((), ())), preferred_element_type=jnp.float32)

    tile = order // 2

    def right(b, source):
        def body(m, _):
            at = pl.ds(pl.multiple_of(m * tile, tile), tile)
            real_in, imag_in = source(at)
            real = nt(real_in, whole[b, 0]) - nt(imag_in, whole[b, 1])
            real = real.astype(jnp.bfloat16)
            hcat[at, :order] = real
            hneg[at, order:] = real
            imag = nt(real_in, whole[b, 1]) + nt(imag_in, whole[b, 0])
            imag = imag.astype(jnp.bfloat16)
            hcat[at, order:] = imag
            hneg[at, :order] = -imag
            return 0

        lax.fori_loop(0, order // tile, body, 0)

    def left(b, at):
        return nn(whole[b, 0, at, :], hcat[...]) + nn(whole[b, 1, at, :], hneg[...])

    send_own(1)
    send_own(0)
    stem_copy.wait()
    own_copies[1].wait()
    collect(1, 0)
    send_own(3)
    right(1, lambda at: (stem_v[0, at, :], stem_v[1, at, :]))
    own_copies[0].wait()
    collect(0, 0)
    send_own(2)

    def left_first(m, _):
        at = pl.ds(pl.multiple_of(m * tile, tile), tile)
        step_v[at, :] = left(0, at).astype(jnp.bfloat16)
        return 0

    lax.fori_loop(0, order // tile, left_first, 0)

    def rows_of(p):
        return pl.ds(pl.multiple_of(p * share, share), share)

    def mid_copy(d, to, at):
        return pltpu.make_async_remote_copy(
            src_ref=step_v.at[rows_of(to), :], dst_ref=moved.at[rows_of(at), :],
            send_sem=mid_send.at[d - 1], recv_sem=mid_recv.at[d - 1],
            device_id={"row": to}, device_id_type=MESH)

    for d in range(1, rows):
        mid_copy(d, lax.rem(me + d, rows), me).start()
    mid_own_copy = pltpu.make_async_copy(step_v.at[rows_of(me), :], moved.at[rows_of(me), :], mid_own)
    mid_own_copy.start()

    own_copies[3].wait()
    collect(3, 0)
    for d in range(1, rows):
        mid_copy(d, lax.rem(me + d, rows), lax.rem(me + rows - d, rows)).wait_recv()
    mid_own_copy.wait()
    right(3, lambda at: (moved[at, :order], moved[at, order:]))

    own_copies[2].wait()
    tail = order // TAIL_CHUNKS
    lane = lax.broadcasted_iota(jnp.int32, (tail, LANES), 1)
    low = lane < share

    def fin_copy(t, d, to, at):
        span = slice(t * tail, (t + 1) * tail)
        return pltpu.make_async_remote_copy(
            src_ref=leave.at[to, span, :], dst_ref=fin.at[at, span, :],
            send_sem=fin_send.at[t, d - 1], recv_sem=fin_recv.at[t, d - 1],
            device_id={"row": to}, device_id_type=MESH)

    def fin_own_copy(t):
        span = slice(t * tail, (t + 1) * tail)
        return pltpu.make_async_copy(leave.at[me, span, :], fin.at[me, span, :], fin_own.at[t])

    per = CHUNKS[2] // TAIL_CHUNKS
    for t in range(TAIL_CHUNKS):
        for ch in range(t * per, (t + 1) * per):
            collect(2, ch)
        at = pl.ds(t * tail, tail)
        made = left(2, at)
        for pair in range(rows // 2):
            real = made[:, pair * LANES:(pair + 1) * LANES]
            imag = made[:, order + pair * LANES:order + (pair + 1) * LANES]
            first = jnp.where(low, real, pltpu.roll(imag, share, 1))
            second = jnp.where(low, pltpu.roll(real, share, 1), imag)
            leave[2 * pair, at, :] = first.astype(jnp.bfloat16)
            leave[2 * pair + 1, at, :] = second.astype(jnp.bfloat16)
        for d in range(1, rows):
            fin_copy(t, d, lax.rem(me + d, rows), me).start()
        fin_own_copy(t).start()

    for t in range(TAIL_CHUNKS):
        at = pl.ds(t * tail, tail)
        fin_own_copy(t).wait()
        for d in range(1, rows):
            fin_copy(t, d, lax.rem(me + d, rows), lax.rem(me + rows - d, rows)).wait_recv()
        for pair in range(rows // 2):
            first = fin[2 * pair, at, :].astype(jnp.float32)
            second = fin[2 * pair + 1, at, :].astype(jnp.float32)
            lanes = slice(pair * LANES, (pair + 1) * LANES)
            real = jnp.where(low, first, pltpu.roll(second, share, 1))
            imag = jnp.where(low, pltpu.roll(first, share, 1), second)
            out_ref[0, at, lanes] = real.astype(jnp.bfloat16)
            out_ref[1, at, lanes] = imag.astype(jnp.bfloat16)

    for b in BRANCH_ORDER:
        for ch in range(CHUNKS[b]):
            for k in range(cols - 1):
                @pl.when((z - k >= 0) & has_up)
                def _():
                    up_copy(b, ch, k, z - k).wait_send()

                @pl.when((z + k <= cols - 1) & has_dn)
                def _():
                    dn_copy(b, ch, k, z + k).wait_send()
    for d in range(1, rows):
        mid_copy(d, lax.rem(me + d, rows), me).wait_send()
        for t in range(TAIL_CHUNKS):
            fin_copy(t, d, lax.rem(me + d, rows), me).wait_send()


def fused(stem, branch):
    order = stem.shape[3]
    rows = lax.axis_size("row")
    cols = lax.axis_size("col")
    split = jnp.transpose(stem[0, 0, 0], (1, 0, 2))
    bf16 = jnp.bfloat16
    dma = pltpu.SemaphoreType.DMA
    hops = max(cols - 1, 1)
    result = pl.pallas_call(
        functools.partial(kernel, rows, cols),
        out_shape=jax.ShapeDtypeStruct((2, order, order), bf16),
        in_specs=[pl.BlockSpec(memory_space=pl.ANY)] * 2,
        out_specs=pl.BlockSpec(memory_space=pltpu.VMEM),
        scratch_shapes=[
            pltpu.VMEM((2, order, order), bf16),
            pltpu.VMEM((4, 2, order, order), bf16),
            pltpu.VMEM((order, 2 * order), bf16),
            pltpu.VMEM((order, 2 * order), bf16),
            pltpu.VMEM((order, 2 * order), bf16),
            pltpu.VMEM((order, 2 * order), bf16),
            pltpu.VMEM((rows, order, LANES), bf16),
            pltpu.VMEM((rows, order, LANES), bf16),
            dma((4, MAX_CHUNKS, hops)), dma((4, MAX_CHUNKS, hops)),
            dma((4, MAX_CHUNKS, hops)), dma((4, MAX_CHUNKS, hops)),
            dma((4,)), dma,
            dma((rows - 1,)), dma((rows - 1,)), dma,
            dma((TAIL_CHUNKS, rows - 1)), dma((TAIL_CHUNKS, rows - 1)), dma((TAIL_CHUNKS,)),
        ],
        compiler_params=pltpu.CompilerParams(
            collective_id=0, has_side_effects=True, vmem_limit_bytes=48 * 1024 * 1024),
    )(split, branch[0])
    return jnp.transpose(result, (1, 0, 2))[None, None, None]


def right_piece(block, piece):
    width = piece.shape[2]
    items = block.shape[0]
    order_size = block.shape[1]
    flat = block.reshape(items * order_size, 2 * width)
    real_t = piece[0].T
    imag_t = piece[1].T
    weight = jnp.block([[real_t, imag_t], [-imag_t, real_t]])
    product = jnp.dot(flat, weight, preferred_element_type=jnp.float32)
    return product.reshape(items, order_size, 2, order_size)


def left_piece(block, piece):
    rows_out = piece.shape[1]
    real_in = block[:, :, 0, :]
    imag_in = block[:, :, 1, :]
    real_w = piece[0]
    imag_w = piece[1]
    weight_real = jnp.concatenate([real_w, imag_w], axis=0)
    weight_imag = jnp.concatenate([-imag_w, real_w], axis=0)
    product = jnp.einsum("xi,eij->exj", weight_real, real_in, preferred_element_type=jnp.float32)
    product = product + jnp.einsum(
        "xi,eij->exj", weight_imag, imag_in, preferred_element_type=jnp.float32
    )
    return jnp.stack([product[:, :rows_out, :], product[:, rows_out:, :]], axis=2)


def plain(stem, branch):
    slab_count = stem.shape[2]
    order_size = stem.shape[3]
    row_count = lax.axis_size("row")
    share = order_size // row_count
    whole = lax.all_gather(branch[0], "col", axis=3, tiled=True)
    half_first = right_piece(stem[0, 0], whole[1]).astype(jnp.bfloat16)
    step_first = left_piece(half_first, whole[0]).astype(jnp.bfloat16)
    outgoing = step_first.reshape(slab_count, row_count, share, 2, order_size)
    moved = lax.all_to_all(outgoing, "row", split_axis=1, concat_axis=1, tiled=True)
    flat = moved.reshape(moved.shape[0], order_size, 2, order_size)
    half_second = right_piece(flat, whole[3]).astype(jnp.bfloat16)
    step_second = left_piece(half_second, whole[2]).astype(jnp.bfloat16)
    leaving = step_second.reshape(slab_count, order_size, 2, row_count, share)
    arrived = lax.all_to_all(leaving, "row", split_axis=3, concat_axis=3, tiled=True)
    return arrived.reshape(1, 1, slab_count, order_size, 2, order_size)


def shards(stem, branch):
    order = stem.shape[3]
    rows = lax.axis_size("row")
    fits = (stem.shape[2] == 1 and branch.shape[4] % LANES == 0
            and order % (2 * LANES) == 0 and 2 * (order // rows) == LANES)
    return fused(stem, branch) if fits else plain(stem, branch)


def solution(mesh):
    placed = (P("row", "col", None, None, None, None), P("row", None, None, None, "col"))
    return jax.shard_map(
        shards,
        mesh=mesh,
        in_specs=placed,
        out_specs=P("row", "col", None, None, None, None),
        check_vma=False,
    )
```

```python
import functools

import jax
import jax.numpy as jnp
from jax import lax
from jax.experimental import pallas as pl
from jax.experimental.pallas import tpu as pltpu
from jax.sharding import PartitionSpec as P

MESH = pl.DeviceIdType.MESH
BRANCH_ORDER = (1, 0, 3, 2)
CHUNKS = {1: 1, 0: 1, 3: 1, 2: 4}
MAX_CHUNKS = 4
TAIL_CHUNKS = 4
LANES = 128


def kernel(rows, cols, stem_ref, branch_ref, out_ref,
           stem_v, whole, hcat, hneg, step_v, moved, leave, fin,
           up_send, up_recv, dn_send, dn_recv, own_sem, stem_sem, guest_send, guest_recv,
           mid_send, mid_recv, mid_own, fin_send, fin_recv, fin_own):
    order = stem_ref.shape[1]
    width = branch_ref.shape[3]
    share = order // rows
    me = lax.axis_index("row")
    z = lax.axis_index("col")
    odd = lax.rem(me, 2) == 1
    partner = z + 1 - 2 * lax.rem(z, 2)
    end = (z == 0) | (z == cols - 1)
    lends = end & odd
    hosts = jnp.logical_not(end) & odd
    works = jnp.logical_not(lends)
    units = works.astype(jnp.int32) + hosts.astype(jnp.int32)
    has_up = z < cols - 1
    has_dn = z > 0
    feeds_up = has_up & jnp.logical_not((z == cols - 2) & odd)
    feeds_dn = has_dn & jnp.logical_not((z == 1) & odd)

    stem_copy = pltpu.make_async_copy(stem_ref, stem_v.at[0], stem_sem)
    stem_copy.start()
    own_copies = {}
    own_lanes = pl.ds(pl.multiple_of(z * width, width), width)
    for b in BRANCH_ORDER:
        own_copies[b] = pltpu.make_async_copy(branch_ref.at[b], whole.at[b, :, :, own_lanes], own_sem.at[b])
        own_copies[b].start()

    barrier = pltpu.get_barrier_semaphore()
    for d in range(1, rows):
        peer = lax.rem(me + d, rows)
        pl.semaphore_signal(barrier, inc=1, device_id={"row": peer}, device_id_type=MESH)
        pl.semaphore_signal(barrier, inc=1, device_id={"row": peer, "col": partner}, device_id_type=MESH)

    @pl.when(has_up)
    def _():
        pl.semaphore_signal(barrier, inc=1, device_id={"col": z + 1}, device_id_type=MESH)

    @pl.when(has_dn)
    def _():
        pl.semaphore_signal(barrier, inc=1, device_id={"col": z - 1}, device_id_type=MESH)

    pl.semaphore_wait(barrier, 2 * (rows - 1) + has_up.astype(jnp.int32) + has_dn.astype(jnp.int32))

    def block_at(b, ch, origin):
        step = order // CHUNKS[b]
        lanes = pl.ds(pl.multiple_of(origin * width, width), width)
        return whole.at[b, :, ch * step:(ch + 1) * step, lanes]

    def own_at(b, ch):
        step = order // CHUNKS[b]
        return branch_ref.at[b, :, ch * step:(ch + 1) * step, :]

    def up_copy(b, ch, k, origin, own=False):
        return pltpu.make_async_remote_copy(
            src_ref=own_at(b, ch) if own else block_at(b, ch, origin), dst_ref=block_at(b, ch, origin),
            send_sem=up_send.at[b, ch, k], recv_sem=up_recv.at[b, ch, k],
            device_id={"col": z + 1}, device_id_type=MESH)

    def dn_copy(b, ch, k, origin, own=False):
        return pltpu.make_async_remote_copy(
            src_ref=own_at(b, ch) if own else block_at(b, ch, origin), dst_ref=block_at(b, ch, origin),
            send_sem=dn_send.at[b, ch, k], recv_sem=dn_recv.at[b, ch, k],
            device_id={"col": z - 1}, device_id_type=MESH)

    def send_own(b):
        for ch in range(CHUNKS[b]):
            @pl.when(feeds_up)
            def _():
                up_copy(b, ch, 0, z, own=True).start()

            @pl.when(feeds_dn)
            def _():
                dn_copy(b, ch, 0, z, own=True).start()

    def collect(b, ch):
        for k in range(cols - 1):
            @pl.when((z - 1 - k >= 0) & works)
            def _():
                up_copy(b, ch, k, z - 1 - k).wait_recv()
                if k + 1 < cols - 1:
                    @pl.when(feeds_up)
                    def _():
                        up_copy(b, ch, k + 1, z - 1 - k).start()

            @pl.when((z + 1 + k <= cols - 1) & works)
            def _():
                dn_copy(b, ch, k, z + 1 + k).wait_recv()
                if k + 1 < cols - 1:
                    @pl.when(feeds_dn)
                    def _():
                        dn_copy(b, ch, k + 1, z + 1 + k).start()

    def nt(a, w):
        return lax.dot_general(a, w, (((1,), (1,)), ((), ())), preferred_element_type=jnp.float32)

    def nn(w, a):
        return lax.dot_general(w, a, (((1,), (0,)), ((), ())), preferred_element_type=jnp.float32)

    halves = 2
    tile = order // halves

    def over_units(make):
        def body(i, _):
            m = lax.rem(i, halves)
            make(i // halves, pl.ds(pl.multiple_of(m * tile, tile), tile))
            return 0

        lax.fori_loop(0, units * halves, body, 0)

    def right(b, source):
        def make(u, at):
            real_in, imag_in = source(u, at)
            real = nt(real_in, whole[b, 0]) - nt(imag_in, whole[b, 1])
            real = real.astype(jnp.bfloat16)
            hcat[u, at, :order] = real
            hneg[u, at, order:] = real
            imag = nt(real_in, whole[b, 1]) + nt(imag_in, whole[b, 0])
            imag = imag.astype(jnp.bfloat16)
            hcat[u, at, order:] = imag
            hneg[u, at, :order] = -imag

        over_units(make)

    def left(b, u, at):
        return nn(whole[b, 0, at, :], hcat[u]) + nn(whole[b, 1, at, :], hneg[u])

    guest_copy = pltpu.make_async_remote_copy(
        src_ref=stem_ref, dst_ref=stem_v.at[1], send_sem=guest_send, recv_sem=guest_recv,
        device_id={"col": partner}, device_id_type=MESH)

    send_own(1)

    @pl.when(lends)
    def _():
        guest_copy.start()

    send_own(0)
    stem_copy.wait()
    own_copies[1].wait()
    collect(1, 0)
    send_own(3)

    @pl.when(hosts)
    def _():
        guest_copy.wait_recv()

    right(1, lambda u, at: (stem_v[u, 0, at, :], stem_v[u, 1, at, :]))
    own_copies[0].wait()
    collect(0, 0)
    send_own(2)

    def left_first(u, at):
        step_v[u, at, :] = left(0, u, at).astype(jnp.bfloat16)

    over_units(left_first)

    def rows_of(p):
        return pl.ds(pl.multiple_of(p * share, share), share)

    def active(u):
        return works if u == 0 else hosts

    def mid_copy(u, d):
        to = lax.rem(me + d, rows)
        q = z if u == 0 else partner
        lent = ((q == 0) | (q == cols - 1)) & (lax.rem(to, 2) == 1)
        slot = lent.astype(jnp.int32)
        home = z + slot * (partner - z) if u == 0 else partner + slot * (z - partner)
        return pltpu.make_async_remote_copy(
            src_ref=step_v.at[u, rows_of(to), :], dst_ref=moved.at[slot, rows_of(me), :],
            send_sem=mid_send.at[u, d - 1], recv_sem=mid_recv.at[slot, d - 1],
            device_id={"row": to, "col": home}, device_id_type=MESH)

    def mid_arrival(u, d):
        origin = lax.rem(me + rows - d, rows)
        return pltpu.make_async_remote_copy(
            src_ref=step_v.at[u, rows_of(origin), :], dst_ref=moved.at[u, rows_of(origin), :],
            send_sem=mid_send.at[u, d - 1], recv_sem=mid_recv.at[u, d - 1],
            device_id={"row": origin}, device_id_type=MESH)

    def mid_own_copy(u):
        return pltpu.make_async_copy(step_v.at[u, rows_of(me), :], moved.at[u, rows_of(me), :], mid_own.at[u])

    for u in (1, 0):
        @pl.when(active(u))
        def _():
            for d in range(1, rows):
                mid_copy(u, d).start()
            mid_own_copy(u).start()

    own_copies[3].wait()
    collect(3, 0)
    for u in (0, 1):
        @pl.when(active(u))
        def _():
            for d in range(1, rows):
                mid_arrival(u, d).wait_recv()
            mid_own_copy(u).wait()

    right(3, lambda u, at: (moved[u, at, :order], moved[u, at, order:]))

    own_copies[2].wait()
    tail = order // TAIL_CHUNKS
    lane = lax.broadcasted_iota(jnp.int32, (tail, LANES), 1)
    low = lane < share

    def fin_copy(u, t, d):
        span = slice(t * tail, (t + 1) * tail)
        to = lax.rem(me + d, rows)
        return pltpu.make_async_remote_copy(
            src_ref=leave.at[u, to, span, :], dst_ref=fin.at[me, span, :],
            send_sem=fin_send.at[u, t, d], recv_sem=fin_recv.at[t, d],
            device_id={"row": to, "col": z if u == 0 else partner}, device_id_type=MESH)

    def fin_arrival(t, d):
        span = slice(t * tail, (t + 1) * tail)
        origin = lax.rem(me + rows - d, rows)
        return pltpu.make_async_remote_copy(
            src_ref=leave.at[0, origin, span, :], dst_ref=fin.at[origin, span, :],
            send_sem=fin_send.at[0, t, d], recv_sem=fin_recv.at[t, d],
            device_id={"row": origin, "col": partner}, device_id_type=MESH)

    def fin_own_copy(t):
        span = slice(t * tail, (t + 1) * tail)
        return pltpu.make_async_copy(leave.at[0, me, span, :], fin.at[me, span, :], fin_own.at[t])

    for t in range(TAIL_CHUNKS):
        collect(2, t)
        at = pl.ds(t * tail, tail)
        for u in (1, 0):
            @pl.when(active(u))
            def _():
                made = left(2, u, at)
                for pair in range(rows // 2):
                    real = made[:, pair * LANES:(pair + 1) * LANES]
                    imag = made[:, order + pair * LANES:order + (pair + 1) * LANES]
                    first = jnp.where(low, real, pltpu.roll(imag, share, 1))
                    second = jnp.where(low, pltpu.roll(real, share, 1), imag)
                    leave[u, 2 * pair, at, :] = first.astype(jnp.bfloat16)
                    leave[u, 2 * pair + 1, at, :] = second.astype(jnp.bfloat16)
                for d in range(u == 0, rows):
                    fin_copy(u, t, d).start()
                if u == 0:
                    fin_own_copy(t).start()

    for t in range(TAIL_CHUNKS):
        at = pl.ds(t * tail, tail)

        @pl.when(works)
        def _():
            fin_own_copy(t).wait()

        @pl.when(lends)
        def _():
            fin_arrival(t, 0).wait_recv()

        for d in range(1, rows):
            fin_arrival(t, d).wait_recv()
        for pair in range(rows // 2):
            first = fin[2 * pair, at, :].astype(jnp.float32)
            second = fin[2 * pair + 1, at, :].astype(jnp.float32)
            lanes = slice(pair * LANES, (pair + 1) * LANES)
            real = jnp.where(low, first, pltpu.roll(second, share, 1))
            imag = jnp.where(low, pltpu.roll(first, share, 1), second)
            out_ref[0, at, lanes] = real.astype(jnp.bfloat16)
            out_ref[1, at, lanes] = imag.astype(jnp.bfloat16)

    for b in BRANCH_ORDER:
        for ch in range(CHUNKS[b]):
            for k in range(cols - 1):
                @pl.when((z - k >= 0) & feeds_up)
                def _():
                    up_copy(b, ch, k, z - k).wait_send()

                @pl.when((z + k <= cols - 1) & feeds_dn)
                def _():
                    dn_copy(b, ch, k, z + k).wait_send()

    @pl.when(lends)
    def _():
        guest_copy.wait_send()

    for u in (0, 1):
        @pl.when(active(u))
        def _():
            for d in range(1, rows):
                mid_copy(u, d).wait_send()
            for t in range(TAIL_CHUNKS):
                for d in range(u == 0, rows):
                    fin_copy(u, t, d).wait_send()


def fused(stem, branch):
    order = stem.shape[3]
    rows = lax.axis_size("row")
    cols = lax.axis_size("col")
    split = jnp.transpose(stem[0, 0, 0], (1, 0, 2))
    bf16 = jnp.bfloat16
    dma = pltpu.SemaphoreType.DMA
    hops = dma((4, MAX_CHUNKS, cols - 1))
    result = pl.pallas_call(
        functools.partial(kernel, rows, cols),
        out_shape=jax.ShapeDtypeStruct((2, order, order), bf16),
        in_specs=[pl.BlockSpec(memory_space=pl.ANY)] * 2,
        out_specs=pl.BlockSpec(memory_space=pltpu.VMEM),
        scratch_shapes=[
            pltpu.VMEM((2, 2, order, order), bf16),
            pltpu.VMEM((4, 2, order, order), bf16),
            pltpu.VMEM((2, order, 2 * order), bf16),
            pltpu.VMEM((2, order, 2 * order), bf16),
            pltpu.VMEM((2, order, 2 * order), bf16),
            pltpu.VMEM((2, order, 2 * order), bf16),
            pltpu.VMEM((2, rows, order, LANES), bf16),
            pltpu.VMEM((rows, order, LANES), bf16),
            hops, hops, hops, hops,
            dma((4,)), dma, dma, dma,
            dma((2, rows - 1)), dma((2, rows - 1)), dma((2,)),
            dma((2, TAIL_CHUNKS, rows)), dma((TAIL_CHUNKS, rows)), dma((TAIL_CHUNKS,)),
        ],
        compiler_params=pltpu.CompilerParams(
            collective_id=0, has_side_effects=True, vmem_limit_bytes=48 * 1024 * 1024),
    )(split, branch[0])
    return jnp.transpose(result, (1, 0, 2))[None, None, None]


def right_piece(block, piece):
    width = piece.shape[2]
    items = block.shape[0]
    order_size = block.shape[1]
    flat = block.reshape(items * order_size, 2 * width)
    real_t = piece[0].T
    imag_t = piece[1].T
    weight = jnp.block([[real_t, imag_t], [-imag_t, real_t]])
    product = jnp.dot(flat, weight, preferred_element_type=jnp.float32)
    return product.reshape(items, order_size, 2, order_size)


def left_piece(block, piece):
    rows_out = piece.shape[1]
    real_in = block[:, :, 0, :]
    imag_in = block[:, :, 1, :]
    real_w = piece[0]
    imag_w = piece[1]
    weight_real = jnp.concatenate([real_w, imag_w], axis=0)
    weight_imag = jnp.concatenate([-imag_w, real_w], axis=0)
    product = jnp.einsum("xi,eij->exj", weight_real, real_in, preferred_element_type=jnp.float32)
    product = product + jnp.einsum(
        "xi,eij->exj", weight_imag, imag_in, preferred_element_type=jnp.float32
    )
    return jnp.stack([product[:, :rows_out, :], product[:, rows_out:, :]], axis=2)


def plain(stem, branch):
    slab_count = stem.shape[2]
    order_size = stem.shape[3]
    row_count = lax.axis_size("row")
    share = order_size // row_count
    whole = lax.all_gather(branch[0], "col", axis=3, tiled=True)
    half_first = right_piece(stem[0, 0], whole[1]).astype(jnp.bfloat16)
    step_first = left_piece(half_first, whole[0]).astype(jnp.bfloat16)
    outgoing = step_first.reshape(slab_count, row_count, share, 2, order_size)
    moved = lax.all_to_all(outgoing, "row", split_axis=1, concat_axis=1, tiled=True)
    flat = moved.reshape(moved.shape[0], order_size, 2, order_size)
    half_second = right_piece(flat, whole[3]).astype(jnp.bfloat16)
    step_second = left_piece(half_second, whole[2]).astype(jnp.bfloat16)
    leaving = step_second.reshape(slab_count, order_size, 2, row_count, share)
    arrived = lax.all_to_all(leaving, "row", split_axis=3, concat_axis=3, tiled=True)
    return arrived.reshape(1, 1, slab_count, order_size, 2, order_size)


def shards(stem, branch):
    order = stem.shape[3]
    rows = lax.axis_size("row")
    fits = (stem.shape[2] == 1 and lax.axis_size("col") == 4 and branch.shape[4] % LANES == 0
            and order % (2 * LANES) == 0 and 2 * (order // rows) == LANES)
    return fused(stem, branch) if fits else plain(stem, branch)


def solution(mesh):
    placed = (P("row", "col", None, None, None, None), P("row", None, None, None, "col"))
    return jax.shard_map(
        shards,
        mesh=mesh,
        in_specs=placed,
        out_specs=P("row", "col", None, None, None, None),
        check_vma=False,
    )
```

```python
import functools

import jax
import jax.numpy as jnp
from jax import lax
from jax.experimental import pallas as pl
from jax.experimental.pallas import tpu as pltpu
from jax.sharding import PartitionSpec as P

MESH = pl.DeviceIdType.MESH
BRANCH_ORDER = (1, 0, 3, 2)
CHUNKS = {1: 1, 0: 1, 3: 1, 2: 4}
MAX_CHUNKS = 4
TAIL_CHUNKS = 4
LANES = 128


def kernel(rows, cols, stem_ref, branch_ref, out_ref,
           stem_v, whole, hcat, hneg, step_v, moved, leave, fin,
           up_send, up_recv, dn_send, dn_recv, own_sem, stem_sem, guest_send, guest_recv,
           mid_send, mid_recv, mid_own, fin_send, fin_recv, fin_own):
    order = stem_ref.shape[1]
    width = branch_ref.shape[3]
    share = order // rows
    me = lax.axis_index("row")
    z = lax.axis_index("col")
    odd = lax.rem(me, 2) == 1
    partner = z + 1 - 2 * lax.rem(z, 2)
    end = (z == 0) | (z == cols - 1)
    lends = end & odd
    hosts = jnp.logical_not(end) & odd
    works = jnp.logical_not(lends)
    units = works.astype(jnp.int32) + hosts.astype(jnp.int32)
    has_up = z < cols - 1
    has_dn = z > 0
    feeds_up = has_up & jnp.logical_not((z == cols - 2) & odd)
    feeds_dn = has_dn & jnp.logical_not((z == 1) & odd)

    stem_copy = pltpu.make_async_copy(stem_ref, stem_v.at[0], stem_sem)
    stem_copy.start()
    own_copies = {}
    own_lanes = pl.ds(pl.multiple_of(z * width, width), width)
    for b in BRANCH_ORDER:
        own_copies[b] = pltpu.make_async_copy(branch_ref.at[b], whole.at[b, :, :, own_lanes], own_sem.at[b])
        own_copies[b].start()

    barrier = pltpu.get_barrier_semaphore()
    for d in range(1, rows):
        peer = lax.rem(me + d, rows)
        pl.semaphore_signal(barrier, inc=1, device_id={"row": peer}, device_id_type=MESH)
        pl.semaphore_signal(barrier, inc=1, device_id={"row": peer, "col": partner}, device_id_type=MESH)

    @pl.when(has_up)
    def _():
        pl.semaphore_signal(barrier, inc=1, device_id={"col": z + 1}, device_id_type=MESH)

    @pl.when(has_dn)
    def _():
        pl.semaphore_signal(barrier, inc=1, device_id={"col": z - 1}, device_id_type=MESH)

    pl.semaphore_wait(barrier, 2 * (rows - 1) + has_up.astype(jnp.int32) + has_dn.astype(jnp.int32))

    def block_at(b, ch, origin):
        step = order // CHUNKS[b]
        lanes = pl.ds(pl.multiple_of(origin * width, width), width)
        return whole.at[b, :, ch * step:(ch + 1) * step, lanes]

    def own_at(b, ch):
        step = order // CHUNKS[b]
        return branch_ref.at[b, :, ch * step:(ch + 1) * step, :]

    def up_copy(b, ch, k, origin, own=False):
        return pltpu.make_async_remote_copy(
            src_ref=own_at(b, ch) if own else block_at(b, ch, origin), dst_ref=block_at(b, ch, origin),
            send_sem=up_send.at[b, ch, k], recv_sem=up_recv.at[b, ch, k],
            device_id={"col": z + 1}, device_id_type=MESH)

    def dn_copy(b, ch, k, origin, own=False):
        return pltpu.make_async_remote_copy(
            src_ref=own_at(b, ch) if own else block_at(b, ch, origin), dst_ref=block_at(b, ch, origin),
            send_sem=dn_send.at[b, ch, k], recv_sem=dn_recv.at[b, ch, k],
            device_id={"col": z - 1}, device_id_type=MESH)

    def send_own(b, who):
        for ch in range(CHUNKS[b]):
            @pl.when(feeds_up & who)
            def _():
                up_copy(b, ch, 0, z, own=True).start()

            @pl.when(feeds_dn & who)
            def _():
                dn_copy(b, ch, 0, z, own=True).start()

    def sent_own(b, who):
        for ch in range(CHUNKS[b]):
            @pl.when(feeds_up & who)
            def _():
                up_copy(b, ch, 0, z, own=True).wait_send()

            @pl.when(feeds_dn & who)
            def _():
                dn_copy(b, ch, 0, z, own=True).wait_send()

    def collect_hop(b, ch, k):
        @pl.when((z - 1 - k >= 0) & works)
        def _():
            up_copy(b, ch, k, z - 1 - k).wait_recv()
            if k + 1 < cols - 1:
                @pl.when(feeds_up)
                def _():
                    up_copy(b, ch, k + 1, z - 1 - k).start()

        @pl.when((z + 1 + k <= cols - 1) & works)
        def _():
            dn_copy(b, ch, k, z + 1 + k).wait_recv()
            if k + 1 < cols - 1:
                @pl.when(feeds_dn)
                def _():
                    dn_copy(b, ch, k + 1, z + 1 + k).start()

    def nt(a, w):
        return lax.dot_general(a, w, (((1,), (1,)), ((), ())), preferred_element_type=jnp.float32)

    def nn(w, a):
        return lax.dot_general(w, a, (((1,), (0,)), ((), ())), preferred_element_type=jnp.float32)

    halves = 2
    tile = order // halves

    def over_units(make):
        def body(i, _):
            m = lax.rem(i, halves)
            make(i // halves, pl.ds(pl.multiple_of(m * tile, tile), tile))
            return 0

        lax.fori_loop(0, units * halves, body, 0)

    def right(b, source):
        def make(u, at):
            real_in, imag_in = source(u, at)
            real = nt(real_in, whole[b, 0]) - nt(imag_in, whole[b, 1])
            real = real.astype(jnp.bfloat16)
            hcat[u, at, :order] = real
            hneg[u, at, order:] = real
            imag = nt(real_in, whole[b, 1]) + nt(imag_in, whole[b, 0])
            imag = imag.astype(jnp.bfloat16)
            hcat[u, at, order:] = imag
            hneg[u, at, :order] = -imag

        over_units(make)

    def left(b, u, at):
        return nn(whole[b, 0, at, :], hcat[u]) + nn(whole[b, 1, at, :], hneg[u])

    guest_copy = pltpu.make_async_remote_copy(
        src_ref=stem_ref, dst_ref=stem_v.at[1], send_sem=guest_send, recv_sem=guest_recv,
        device_id={"col": partner}, device_id_type=MESH)

    middle = jnp.logical_not(end)
    keeps = end & works
    always = z >= 0
    send_own(1, always)
    send_own(0, always)

    sent_own(1, lends)

    @pl.when(lends)
    def _():
        guest_copy.start()

    sent_own(0, lends)

    @pl.when(lends)
    def _():
        guest_copy.wait_send()

    send_own(3, lends)
    sent_own(3, lends)
    send_own(2, lends)
    sent_own(2, lends)

    stem_copy.wait()
    own_copies[1].wait()
    own_copies[0].wait()
    collect_hop(1, 0, 0)
    send_own(3, middle)
    collect_hop(0, 0, 0)
    collect_hop(1, 0, 1)
    send_own(2, middle)
    send_own(3, keeps)
    collect_hop(1, 0, 2)
    collect_hop(0, 0, 1)
    send_own(2, keeps)
    collect_hop(0, 0, 2)

    @pl.when(hosts)
    def _():
        guest_copy.wait_recv()

    right(1, lambda u, at: (stem_v[u, 0, at, :], stem_v[u, 1, at, :]))

    def left_first(u, at):
        step_v[u, at, :] = left(0, u, at).astype(jnp.bfloat16)

    over_units(left_first)

    def rows_of(p):
        return pl.ds(pl.multiple_of(p * share, share), share)

    def active(u):
        return works if u == 0 else hosts

    def mid_copy(u, d):
        to = lax.rem(me + d, rows)
        q = z if u == 0 else partner
        lent = ((q == 0) | (q == cols - 1)) & (lax.rem(to, 2) == 1)
        slot = lent.astype(jnp.int32)
        home = z + slot * (partner - z) if u == 0 else partner + slot * (z - partner)
        return pltpu.make_async_remote_copy(
            src_ref=step_v.at[u, rows_of(to), :], dst_ref=moved.at[slot, rows_of(me), :],
            send_sem=mid_send.at[u, d - 1], recv_sem=mid_recv.at[slot, d - 1],
            device_id={"row": to, "col": home}, device_id_type=MESH)

    def mid_arrival(u, d):
        origin = lax.rem(me + rows - d, rows)
        return pltpu.make_async_remote_copy(
            src_ref=step_v.at[u, rows_of(origin), :], dst_ref=moved.at[u, rows_of(origin), :],
            send_sem=mid_send.at[u, d - 1], recv_sem=mid_recv.at[u, d - 1],
            device_id={"row": origin}, device_id_type=MESH)

    def mid_own_copy(u):
        return pltpu.make_async_copy(step_v.at[u, rows_of(me), :], moved.at[u, rows_of(me), :], mid_own.at[u])

    for u in (1, 0):
        @pl.when(active(u))
        def _():
            for d in range(1, rows):
                mid_copy(u, d).start()
            mid_own_copy(u).start()

    own_copies[3].wait()
    collect_hop(3, 0, 0)
    for t in range(TAIL_CHUNKS):
        collect_hop(2, t, 0)
    collect_hop(3, 0, 1)
    collect_hop(3, 0, 2)
    for u in (0, 1):
        @pl.when(active(u))
        def _():
            for d in range(1, rows):
                mid_arrival(u, d).wait_recv()
            mid_own_copy(u).wait()

    right(3, lambda u, at: (moved[u, at, :order], moved[u, at, order:]))

    own_copies[2].wait()
    tail = order // TAIL_CHUNKS
    lane = lax.broadcasted_iota(jnp.int32, (tail, LANES), 1)
    low = lane < share

    def fin_copy(u, t, d):
        span = slice(t * tail, (t + 1) * tail)
        to = lax.rem(me + d, rows)
        return pltpu.make_async_remote_copy(
            src_ref=leave.at[u, to, span, :], dst_ref=fin.at[me, span, :],
            send_sem=fin_send.at[u, t, d], recv_sem=fin_recv.at[t, d],
            device_id={"row": to, "col": z if u == 0 else partner}, device_id_type=MESH)

    def fin_arrival(t, d):
        span = slice(t * tail, (t + 1) * tail)
        origin = lax.rem(me + rows - d, rows)
        return pltpu.make_async_remote_copy(
            src_ref=leave.at[0, origin, span, :], dst_ref=fin.at[origin, span, :],
            send_sem=fin_send.at[0, t, d], recv_sem=fin_recv.at[t, d],
            device_id={"row": origin, "col": partner}, device_id_type=MESH)

    def fin_own_copy(t):
        span = slice(t * tail, (t + 1) * tail)
        return pltpu.make_async_copy(leave.at[0, me, span, :], fin.at[me, span, :], fin_own.at[t])

    for t in range(TAIL_CHUNKS):
        collect_hop(2, t, 1)
        collect_hop(2, t, 2)
        at = pl.ds(t * tail, tail)
        for u in (1, 0):
            @pl.when(active(u))
            def _():
                made = left(2, u, at)
                for pair in range(rows // 2):
                    real = made[:, pair * LANES:(pair + 1) * LANES]
                    imag = made[:, order + pair * LANES:order + (pair + 1) * LANES]
                    first = jnp.where(low, real, pltpu.roll(imag, share, 1))
                    second = jnp.where(low, pltpu.roll(real, share, 1), imag)
                    leave[u, 2 * pair, at, :] = first.astype(jnp.bfloat16)
                    leave[u, 2 * pair + 1, at, :] = second.astype(jnp.bfloat16)
                for d in range(u == 0, rows):
                    fin_copy(u, t, d).start()
                if u == 0:
                    fin_own_copy(t).start()

    for t in range(TAIL_CHUNKS):
        at = pl.ds(t * tail, tail)

        @pl.when(works)
        def _():
            fin_own_copy(t).wait()

        @pl.when(lends)
        def _():
            fin_arrival(t, 0).wait_recv()

        for d in range(1, rows):
            fin_arrival(t, d).wait_recv()
        for pair in range(rows // 2):
            first = fin[2 * pair, at, :].astype(jnp.float32)
            second = fin[2 * pair + 1, at, :].astype(jnp.float32)
            lanes = slice(pair * LANES, (pair + 1) * LANES)
            real = jnp.where(low, first, pltpu.roll(second, share, 1))
            imag = jnp.where(low, pltpu.roll(first, share, 1), second)
            out_ref[0, at, lanes] = real.astype(jnp.bfloat16)
            out_ref[1, at, lanes] = imag.astype(jnp.bfloat16)

    for b in BRANCH_ORDER:
        for ch in range(CHUNKS[b]):
            for k in range(cols - 1):
                @pl.when((z - k >= 0) & feeds_up & works)
                def _():
                    up_copy(b, ch, k, z - k).wait_send()

                @pl.when((z + k <= cols - 1) & feeds_dn & works)
                def _():
                    dn_copy(b, ch, k, z + k).wait_send()

    for u in (0, 1):
        @pl.when(active(u))
        def _():
            for d in range(1, rows):
                mid_copy(u, d).wait_send()
            for t in range(TAIL_CHUNKS):
                for d in range(u == 0, rows):
                    fin_copy(u, t, d).wait_send()


def fused(stem, branch):
    order = stem.shape[3]
    rows = lax.axis_size("row")
    cols = lax.axis_size("col")
    split = jnp.transpose(stem[0, 0, 0], (1, 0, 2))
    bf16 = jnp.bfloat16
    dma = pltpu.SemaphoreType.DMA
    hops = dma((4, MAX_CHUNKS, cols - 1))
    result = pl.pallas_call(
        functools.partial(kernel, rows, cols),
        out_shape=jax.ShapeDtypeStruct((2, order, order), bf16),
        in_specs=[pl.BlockSpec(memory_space=pl.ANY)] * 2,
        out_specs=pl.BlockSpec(memory_space=pltpu.VMEM),
        scratch_shapes=[
            pltpu.VMEM((2, 2, order, order), bf16),
            pltpu.VMEM((4, 2, order, order), bf16),
            pltpu.VMEM((2, order, 2 * order), bf16),
            pltpu.VMEM((2, order, 2 * order), bf16),
            pltpu.VMEM((2, order, 2 * order), bf16),
            pltpu.VMEM((2, order, 2 * order), bf16),
            pltpu.VMEM((2, rows, order, LANES), bf16),
            pltpu.VMEM((rows, order, LANES), bf16),
            hops, hops, hops, hops,
            dma((4,)), dma, dma, dma,
            dma((2, rows - 1)), dma((2, rows - 1)), dma((2,)),
            dma((2, TAIL_CHUNKS, rows)), dma((TAIL_CHUNKS, rows)), dma((TAIL_CHUNKS,)),
        ],
        compiler_params=pltpu.CompilerParams(
            collective_id=0, has_side_effects=True, vmem_limit_bytes=48 * 1024 * 1024),
    )(split, branch[0])
    return jnp.transpose(result, (1, 0, 2))[None, None, None]


def right_piece(block, piece):
    width = piece.shape[2]
    items = block.shape[0]
    order_size = block.shape[1]
    flat = block.reshape(items * order_size, 2 * width)
    real_t = piece[0].T
    imag_t = piece[1].T
    weight = jnp.block([[real_t, imag_t], [-imag_t, real_t]])
    product = jnp.dot(flat, weight, preferred_element_type=jnp.float32)
    return product.reshape(items, order_size, 2, order_size)


def left_piece(block, piece):
    rows_out = piece.shape[1]
    real_in = block[:, :, 0, :]
    imag_in = block[:, :, 1, :]
    real_w = piece[0]
    imag_w = piece[1]
    weight_real = jnp.concatenate([real_w, imag_w], axis=0)
    weight_imag = jnp.concatenate([-imag_w, real_w], axis=0)
    product = jnp.einsum("xi,eij->exj", weight_real, real_in, preferred_element_type=jnp.float32)
    product = product + jnp.einsum(
        "xi,eij->exj", weight_imag, imag_in, preferred_element_type=jnp.float32
    )
    return jnp.stack([product[:, :rows_out, :], product[:, rows_out:, :]], axis=2)


def plain(stem, branch):
    slab_count = stem.shape[2]
    order_size = stem.shape[3]
    row_count = lax.axis_size("row")
    share = order_size // row_count
    whole = lax.all_gather(branch[0], "col", axis=3, tiled=True)
    half_first = right_piece(stem[0, 0], whole[1]).astype(jnp.bfloat16)
    step_first = left_piece(half_first, whole[0]).astype(jnp.bfloat16)
    outgoing = step_first.reshape(slab_count, row_count, share, 2, order_size)
    moved = lax.all_to_all(outgoing, "row", split_axis=1, concat_axis=1, tiled=True)
    flat = moved.reshape(moved.shape[0], order_size, 2, order_size)
    half_second = right_piece(flat, whole[3]).astype(jnp.bfloat16)
    step_second = left_piece(half_second, whole[2]).astype(jnp.bfloat16)
    leaving = step_second.reshape(slab_count, order_size, 2, row_count, share)
    arrived = lax.all_to_all(leaving, "row", split_axis=3, concat_axis=3, tiled=True)
    return arrived.reshape(1, 1, slab_count, order_size, 2, order_size)


def shards(stem, branch):
    order = stem.shape[3]
    rows = lax.axis_size("row")
    fits = (stem.shape[2] == 1 and lax.axis_size("col") == 4 and branch.shape[4] % LANES == 0
            and order % (2 * LANES) == 0 and 2 * (order // rows) == LANES)
    return fused(stem, branch) if fits else plain(stem, branch)


def solution(mesh):
    placed = (P("row", "col", None, None, None, None), P("row", None, None, None, "col"))
    return jax.shard_map(
        shards,
        mesh=mesh,
        in_specs=placed,
        out_specs=P("row", "col", None, None, None, None),
        check_vma=False,
    )
```
